32 devices in a mesh: groups: 2 (over y), pair: 8 (over z, x), aux: 2 (over core).
Axes of the slice: x: 2, y: 2, z: 4, core: 2. Of those that a mesh axis runs over, the one named last changes fastest.
Arguments:
- factors: float32 [8192, 2048], P(('groups', 'pair', 'aux')), parts along dimension 0, may hold values from -0.6 to 0.6
- occupied_energy: float32 [256], P('groups'), parts along dimension 0, may hold values from -3 to -0.4
- virtual_energy: float32 [4096], P('groups'), parts along dimension 0, may hold values from 0.2 to 4
- batch_orbitals: int32 [2], P('groups'), parts along dimension 0, may hold values from 0 to 127, as said below
- panel_order: int32 [32], P('groups'), parts along dimension 0, may hold values from 0 to 31, as said below
Outputs:
- density: float32 [8192, 2048], P(('groups', 'pair', 'aux')), parts along dimension 0
The draws below stay inside these ranges and needn't reach their ends.
There are 2 independent parts, one for each index of `groups`. The reference program is written for one: setup_inputs(seed, part) draws one part's arguments, and reference() takes and returns one part's arrays. A program takes and returns all parts, laid end to end along the dimension named above; each array names one. Nothing has to cross between parts.
Inputs may be any that keep to these rules, and one draw needn't show every extreme that they name: `batch_orbitals`: 1 distinct occupied orbitals. `panel_order`: 16 distinct panel numbers.
All inputs are finite; a program needn't handle non-finite values.
Results may differ from the reference program's by a relative error of at most 0.0001.
Values sent between devices are 32-bit elements; how exact they have to be, the bound alone decides.
A program may use at most 64 MiB of HBM per device.

```python
import jax
import jax.numpy as jnp
from jax import lax

NAUX = 4096
NOCC = 128
NV = 2048
PANEL = 64
NPAN = 16
NI = 1
NCOL = 2048


def pick_distinct(key, total, count):
    remaining = jax.random.permutation(key, total - 1)[:count - 1].astype(jnp.int32)
    chosen = jnp.concatenate([remaining, jnp.full((1,), total - 1, jnp.int32)])
    return jax.random.permutation(jax.random.fold_in(key, 7), chosen).astype(jnp.int32)


def draw_batch_orbitals(key, part):
    return pick_distinct(jax.random.fold_in(key, 11), NOCC, NI)


def draw_panel_order(key, part):
    return pick_distinct(jax.random.fold_in(key, 23), NCOL // PANEL, NPAN)


def block_levels(rng, shape, split, low, top_value):
    factor_of = 1.0
    for dim, parts in split:
        draws = jax.random.uniform(jax.random.fold_in(jax.random.fold_in(rng, 6), dim), (parts,), jnp.float32, low / len(split), top_value / len(split))
        factor_of = factor_of * jnp.repeat(jnp.exp(draws), shape[dim] // parts).reshape((-1,) + (1,) * (len(shape) - 1 - dim))
    return factor_of


def centred(own_key, extent, spread, reach, split=(), held_as=jnp.bfloat16):
    drawn = spread * jax.random.normal(own_key, extent, jnp.float32)
    if split:
        drawn = drawn * block_levels(own_key, extent, split, -0.22, 0.18)
    return jnp.clip(drawn, -reach, reach).astype(held_as)


def setup_inputs(seed: int = 0, part: int = 0) -> dict:
    key_list = jax.random.split(jax.random.key(seed), 6)
    part_splits = jax.random.split(jax.random.fold_in(key_list[5], part), 6)
    factors = centred(part_splits[0], (NAUX, NCOL), 0.1, 0.6, ((0, 16),), jnp.float32)
    occupied_energy = jnp.clip(jax.random.uniform(part_splits[1], (NOCC,), jnp.float32, -3.0, -0.4), -3.0, -0.4)
    virtual_energy = jnp.clip(jax.random.uniform(part_splits[2], (NV,), jnp.float32, 0.2, 4.0), 0.2, 4.0)
    batch_orbitals = draw_batch_orbitals(jax.random.fold_in(jax.random.fold_in(key_list[5], part), 71), part)
    panel_order = draw_panel_order(jax.random.fold_in(jax.random.fold_in(key_list[5], part), 71), part)
    return dict(factors=factors, occupied_energy=occupied_energy, virtual_energy=virtual_energy, batch_orbitals=batch_orbitals, panel_order=panel_order)


os_scale = 1.3


def reference(factors, occupied_energy, virtual_energy, batch_orbitals, panel_order):
    nvir = virtual_energy.shape[0]
    nbatch = batch_orbitals.shape[0]
    column_energy = jnp.tile(virtual_energy, nbatch) - jnp.repeat(occupied_energy[batch_orbitals], nvir)

    def one_panel(position, density):
        number = panel_order[position]
        first = (number * PANEL).astype(jnp.int32)
        panel_block = lax.dynamic_slice_in_dim(factors, first, PANEL, 1)
        panel_energy = lax.dynamic_slice_in_dim(column_energy, first, PANEL, 0)
        integrals = lax.dot_general(panel_block, factors, (((0,), (0,)), ((), ())),
                                    precision=lax.Precision.HIGHEST, preferred_element_type=jnp.float32)
        amplitudes = os_scale * integrals / (column_energy[None, :] + panel_energy[:, None])
        return density + jnp.dot(panel_block, amplitudes, precision=lax.Precision.HIGHEST,
                                 preferred_element_type=jnp.float32)

    return lax.fori_loop(0, NPAN, one_panel, jnp.zeros(factors.shape, jnp.float32))
```

```python
import jax
import jax.numpy as jnp
from jax import lax
from jax.sharding import PartitionSpec as P

PANEL = 64


os_scale = 1.3


def spread(block, axis, source):
    block = jnp.where(lax.axis_index(axis) == source, block, jnp.zeros_like(block))
    return lax.psum(block, axis)


def column_energies(columns, batch_energy, virtual_energy):
    nvir = virtual_energy.shape[0]
    nbatch = batch_energy.shape[0]
    orbital = columns // nvir
    virtual = columns % nvir
    occ_part = jnp.sum(
        jnp.where(
            orbital[:, None] == jnp.arange(nbatch, dtype=jnp.int32)[None, :],
            batch_energy[None, :],
            0.0,
        ),
        axis=1,
    )
    vir_part = jnp.sum(
        jnp.where(
            virtual[:, None] == jnp.arange(nvir, dtype=jnp.int32)[None, :],
            virtual_energy[None, :],
            0.0,
        ),
        axis=1,
    )
    return vir_part - occ_part


def batch_energies(occupied_energy, batch_orbitals):
    noccupied = occupied_energy.shape[0]
    return jnp.sum(
        jnp.where(
            batch_orbitals[:, None] == jnp.arange(noccupied, dtype=jnp.int32)[None, :],
            occupied_energy[None, :],
            0.0,
        ),
        axis=1,
    )


def by_columns(factors, occupied_energy, virtual_energy, batch_orbitals, panel_order):
    pair_count = lax.axis_size("pair")
    total_columns = factors.shape[1]
    col_local = total_columns // pair_count
    per_owner = col_local // PANEL
    working = lax.all_to_all(factors, "pair", split_axis=1, concat_axis=0, tiled=True)
    batch_energy = batch_energies(occupied_energy, batch_orbitals)
    own_columns = lax.axis_index("pair") * col_local + jnp.arange(col_local, dtype=jnp.int32)
    own_energy = column_energies(own_columns, batch_energy, virtual_energy)

    def one_panel(position, density):
        number = panel_order[position]
        owner_index = number // per_owner
        panel_slab = lax.dynamic_slice_in_dim(working, number % per_owner * PANEL, PANEL, 1)
        panel_block = spread(panel_slab, "pair", owner_index)
        panel_energy = column_energies(
            number * PANEL + jnp.arange(PANEL, dtype=jnp.int32), batch_energy, virtual_energy
        )
        partial_ints = lax.dot_general(
            panel_block,
            working,
            (((0,), (0,)), ((), ())),
            precision=lax.Precision.HIGHEST,
            preferred_element_type=jnp.float32,
        )
        integrals = lax.psum(partial_ints, "aux")
        amplitudes = os_scale * integrals / (own_energy[None, :] + panel_energy[:, None])
        return density + jnp.dot(
            panel_block,
            amplitudes,
            precision=lax.Precision.HIGHEST,
            preferred_element_type=jnp.float32,
        )

    density = lax.fori_loop(
        0, panel_order.shape[0], one_panel, jnp.zeros(working.shape, jnp.float32)
    )
    return lax.all_to_all(density, "pair", split_axis=0, concat_axis=1, tiled=True)


def by_rows(factors, occupied_energy, virtual_energy, batch_orbitals, panel_order):
    total = factors.shape[1]
    batch_energy = batch_energies(occupied_energy, batch_orbitals)
    nvir = virtual_energy.shape[0]
    energy = (virtual_energy[None, :] - batch_energy[:, None]).reshape(-1)
    panels = jnp.concatenate(
        [
            lax.dynamic_slice_in_dim(factors, panel_order[k] * PANEL, PANEL, 1)
            for k in range(panel_order.shape[0])
        ],
        axis=1,
    )
    chosen = jnp.concatenate(
        [
            lax.dynamic_slice_in_dim(energy, panel_order[k] * PANEL, PANEL, 0)
            for k in range(panel_order.shape[0])
        ]
    )
    partial = lax.dot_general(
        panels,
        factors,
        (((0,), (0,)), ((), ())),
        precision=lax.Precision.HIGH,
        preferred_element_type=jnp.float32,
    )
    mine = lax.psum_scatter(partial, ("pair", "aux"), scatter_dimension=0, tiled=True)
    rank = lax.axis_index("pair") * lax.axis_size("aux") + lax.axis_index("aux")
    my_energy = lax.dynamic_slice_in_dim(chosen, rank * mine.shape[0], mine.shape[0], 0)
    mine = os_scale * mine / (energy[None, :] + my_energy[:, None])
    amplitudes = lax.all_gather(mine, ("pair", "aux"), axis=0, tiled=True)
    return jnp.dot(
        panels, amplitudes, precision=lax.Precision.HIGH, preferred_element_type=jnp.float32
    )


def on_device(factors, occupied_energy, virtual_energy, batch_orbitals, panel_order):
    window = panel_order.shape[0] * PANEL
    fits = 4 * window * factors.shape[1] <= 8 * 1024 * 1024
    plan = by_rows if fits else by_columns
    return plan(factors, occupied_energy, virtual_energy, batch_orbitals, panel_order)


def solution(mesh):
    in_specs = (
        P(("groups", "pair", "aux"), None),
        P("groups"),
        P("groups"),
        P("groups"),
        P("groups"),
    )
    out_specs = P(("groups", "pair", "aux"), None)
    return jax.shard_map(
        on_device, mesh=mesh, in_specs=in_specs, out_specs=out_specs, check_vma=False
    )
```

```python
import functools

import jax
import jax.numpy as jnp
from jax import lax
from jax.experimental import pallas as pl
from jax.experimental.pallas import tpu as pltpu
from jax.sharding import PartitionSpec as P

PANEL = 64


os_scale = 1.3


def spread(block, axis, source):
    block = jnp.where(lax.axis_index(axis) == source, block, jnp.zeros_like(block))
    return lax.psum(block, axis)


def column_energies(columns, batch_energy, virtual_energy):
    nvir = virtual_energy.shape[0]
    nbatch = batch_energy.shape[0]
    orbital = columns // nvir
    virtual = columns % nvir
    occ_part = jnp.sum(
        jnp.where(
            orbital[:, None] == jnp.arange(nbatch, dtype=jnp.int32)[None, :],
            batch_energy[None, :],
            0.0,
        ),
        axis=1,
    )
    vir_part = jnp.sum(
        jnp.where(
            virtual[:, None] == jnp.arange(nvir, dtype=jnp.int32)[None, :],
            virtual_energy[None, :],
            0.0,
        ),
        axis=1,
    )
    return vir_part - occ_part


def batch_energies(occupied_energy, batch_orbitals):
    noccupied = occupied_energy.shape[0]
    return jnp.sum(
        jnp.where(
            batch_orbitals[:, None] == jnp.arange(noccupied, dtype=jnp.int32)[None, :],
            occupied_energy[None, :],
            0.0,
        ),
        axis=1,
    )


def by_columns(factors, occupied_energy, virtual_energy, batch_orbitals, panel_order):
    pair_count = lax.axis_size("pair")
    total_columns = factors.shape[1]
    col_local = total_columns // pair_count
    per_owner = col_local // PANEL
    working = lax.all_to_all(factors, "pair", split_axis=1, concat_axis=0, tiled=True)
    batch_energy = batch_energies(occupied_energy, batch_orbitals)
    own_columns = lax.axis_index("pair") * col_local + jnp.arange(col_local, dtype=jnp.int32)
    own_energy = column_energies(own_columns, batch_energy, virtual_energy)

    def one_panel(position, density):
        number = panel_order[position]
        owner_index = number // per_owner
        panel_slab = lax.dynamic_slice_in_dim(working, number % per_owner * PANEL, PANEL, 1)
        panel_block = spread(panel_slab, "pair", owner_index)
        panel_energy = column_energies(
            number * PANEL + jnp.arange(PANEL, dtype=jnp.int32), batch_energy, virtual_energy
        )
        partial_ints = lax.dot_general(
            panel_block,
            working,
            (((0,), (0,)), ((), ())),
            precision=lax.Precision.HIGHEST,
            preferred_element_type=jnp.float32,
        )
        integrals = lax.psum(partial_ints, "aux")
        amplitudes = os_scale * integrals / (own_energy[None, :] + panel_energy[:, None])
        return density + jnp.dot(
            panel_block,
            amplitudes,
            precision=lax.Precision.HIGHEST,
            preferred_element_type=jnp.float32,
        )

    density = lax.fori_loop(
        0, panel_order.shape[0], one_panel, jnp.zeros(working.shape, jnp.float32)
    )
    return lax.all_to_all(density, "pair", split_axis=0, concat_axis=1, tiled=True)


SUB = 2


def split(x):
    high = x.astype(jnp.bfloat16)
    return high, (x - high.astype(jnp.float32)).astype(jnp.bfloat16)


def dot3(a_high, a_low, b_high, b_low):
    dot = functools.partial(jnp.dot, preferred_element_type=jnp.float32)
    return dot(a_high, b_high) + dot(a_high, b_low) + dot(a_low, b_high)


def ring_place(pair, n):
    side = pair % 2
    level = pair // 2
    return level + side * (n - 1 - 2 * level)


def ring_pair(place, n):
    side = place // (n // 2)
    level = place + side * (n - 1 - 2 * place)
    return 2 * level + side


def ring_kernel(
    n, b_ref, p_ref, col_ref, row_ref, out_ref,
    sib_b, sib_p, pt_high, pt_low, p_high, p_low, part, buf, amp,
    sibp_send, sibp_recv, sibb_send, sibb_recv,
    red_send, red_recv, gat_send, gat_recv, siba_send, siba_recv,
):
    depth, total = b_ref.shape
    window = p_ref.shape[1]
    width = total // n
    half = window // 2
    quarter = half // 2
    rows = quarter // SUB
    core = lax.axis_index("aux")
    place = ring_place(lax.axis_index("pair"), n)

    def neighbour(d):
        return {"pair": ring_pair((place + n + 1 - 2 * d) % n, n)}

    sibling = {"aux": 1 - core}

    def columns(q):
        return pl.ds(pl.multiple_of(q * width, width), width)

    def shard(d, step):
        return (place + n * n + (2 * d - 1) * step) % n

    def sib_p_copy():
        return pltpu.make_async_remote_copy(
            p_ref.at[:, pl.ds(pl.multiple_of((1 - core) * half, half), half)], sib_p,
            sibp_send, sibp_recv, device_id=sibling, device_id_type=pl.DeviceIdType.MESH)

    def sib_b_copy(q):
        return pltpu.make_async_remote_copy(
            b_ref.at[:, columns(q)], sib_b.at[:, columns(q)],
            sibb_send.at[q], sibb_recv.at[q], device_id=sibling,
            device_id_type=pl.DeviceIdType.MESH)

    def sub(u):
        return pl.ds(pl.multiple_of(u * rows, rows), rows)

    def amp_rows(d, u):
        return pl.ds(pl.multiple_of(core * half + d * quarter + u * rows, rows), rows)

    def red_copy(d, s, u):
        return pltpu.make_async_remote_copy(
            buf.at[d, s, sub(u)], buf.at[d, s + 1, sub(u)],
            red_send.at[d, s, u], red_recv.at[d, s, u], device_id=neighbour(d),
            device_id_type=pl.DeviceIdType.MESH)

    def gat_copy(d, s, u, q):
        block = amp.at[amp_rows(d, u), columns(q)]
        return pltpu.make_async_remote_copy(
            block, block, gat_send.at[d, s, u], gat_recv.at[d, s, u],
            device_id=neighbour(d), device_id_type=pl.DeviceIdType.MESH)

    def sib_a_copy(d, t, u, q):
        block = amp.at[amp_rows(d, u), columns(q)]
        return pltpu.make_async_remote_copy(
            block, block, siba_send.at[d, t, u], siba_recv.at[d, t, u],
            device_id=sibling, device_id_type=pl.DeviceIdType.MESH)

    def sib_a_arrival(d, t, u, q):
        block = amp.at[
            pl.ds(pl.multiple_of((1 - core) * half + d * quarter + u * rows, rows), rows),
            columns(q)]
        return pltpu.make_async_remote_copy(
            block, block, siba_send.at[d, t, u], siba_recv.at[d, t, u],
            device_id=sibling, device_id_type=pl.DeviceIdType.MESH)

    barrier = pltpu.get_barrier_semaphore()
    for other in (neighbour(0), neighbour(1), sibling):
        pl.semaphore_signal(barrier, inc=1, device_id=other, device_id_type=pl.DeviceIdType.MESH)
    pl.semaphore_wait(barrier, 3)

    sib_p_copy().start()
    for i in range(1, n // 2 + 1):
        sib_b_copy(shard(0, i)).start()
        if i < n // 2:
            sib_b_copy(shard(1, i)).start()
    sib_b_copy(place).start()

    mine = pl.ds(pl.multiple_of(core * half, half), half)
    high, low = split(p_ref[:, mine].T)
    pt_high[:, :depth] = high
    pt_low[:, :depth] = low
    sib_p_copy().wait_recv()
    high, low = split(sib_p[...].T)
    pt_high[:, depth:] = high
    pt_low[:, depth:] = low

    def set_part(d, q):
        lhs = pl.ds(pl.multiple_of(d * quarter, quarter), quarter)
        own_high, own_low = split(b_ref[:, columns(q)])
        sib_high, sib_low = split(sib_b[:, columns(q)])
        part[d] = dot3(pt_high[lhs, :depth], pt_low[lhs, :depth], own_high, own_low) + dot3(
            pt_high[lhs, depth:], pt_low[lhs, depth:], sib_high, sib_low)

    @pl.loop(0, 2)
    def _(d):
        sib_b_copy(shard(d, 1)).wait_recv()
        set_part(d, shard(d, 1))
        buf[d, 0] = part[d]
        for u in range(SUB):
            red_copy(d, 0, u).start()

    for i in range(2, n // 2 + 1):
        sib_b_copy(shard(0, i)).wait_recv()
        if i < n // 2:
            sib_b_copy(shard(1, i)).wait_recv()
    sib_b_copy(place).wait_recv()
    high, low = split(p_ref[...])
    p_high[...] = high
    p_low[...] = low

    @pl.loop(1, n - 1)
    def _(s):
        @pl.loop(0, 2)
        def _(d):
            set_part(d, shard(d, s + 1))
        for u in range(SUB):
            for d in range(2):
                red_copy(d, s - 1, u).wait_recv()
                buf[d, s, sub(u)] += part[d, sub(u)]
                red_copy(d, s, u).start()

    @pl.loop(0, 2)
    def _(d):
        set_part(d, place)
    for u in range(SUB):
        for d in range(2):
            red_copy(d, n - 2, u).wait_recv()
            integrals = buf[d, n - 1, sub(u)] + part[d, sub(u)]
            energy = col_ref[:, columns(place)] + row_ref[amp_rows(d, u), :]
            amp[amp_rows(d, u), columns(place)] = os_scale * integrals / energy
            gat_copy(d, 0, u, place).start()
            sib_a_copy(d, 0, u, place).start()

    def pass_on(s, last):
        for u in range(SUB):
            for d in range(2):
                q = shard(d, s + 1)
                gat_copy(d, s, u, q).wait_recv()
                if not last:
                    gat_copy(d, s + 1, u, q).start()
                sib_a_copy(d, s + 1, u, q).start()

    def density(q):
        total_sum = jnp.zeros((depth, width), jnp.float32)
        for k in range(4):
            span = pl.ds(k * quarter, quarter)
            a_high, a_low = split(amp[span, columns(q)])
            total_sum += dot3(p_high[:, span], p_low[:, span], a_high, a_low)
        out_ref[:, columns(q)] = total_sum

    def finish(d, j):
        q = shard(d, j)
        for u in range(SUB):
            sib_a_arrival(d, j, u, q).wait_recv()
            sib_a_arrival(1 - d, (n - j) % n, u, q).wait_recv()
        density(q)

    middle = n // 2

    @pl.loop(0, middle)
    def _(s):
        pass_on(s, False)

    @pl.loop(0, 2)
    def _(i):
        finish(0, i * middle)

    @pl.loop(middle, n - 2)
    def _(s):
        pass_on(s, False)

        @pl.loop(0, 2)
        def _(d):
            finish(d, n - 1 - s)

    pass_on(n - 2, True)

    @pl.loop(0, 2)
    def _(d):
        finish(d, 1)

    sib_p_copy().wait_send()

    @pl.loop(0, n)
    def _(q):
        sib_b_copy(q).wait_send()

    for d in range(2):
        for u in range(SUB):
            @pl.loop(0, n - 1)
            def _(s):
                red_copy(d, s, u).wait_send()
                gat_copy(d, s, u, shard(d, s)).wait_send()

            @pl.loop(0, n)
            def _(t):
                sib_a_copy(d, t, u, shard(d, t)).wait_send()


def by_rows(factors, occupied_energy, virtual_energy, batch_orbitals, panel_order):
    n = lax.axis_size("pair")
    depth, total = factors.shape
    batch_energy = batch_energies(occupied_energy, batch_orbitals)
    energy = (virtual_energy[None, :] - batch_energy[:, None]).reshape(-1)
    panels = jnp.concatenate(
        [
            lax.dynamic_slice_in_dim(factors, panel_order[k] * PANEL, PANEL, 1)
            for k in range(panel_order.shape[0])
        ],
        axis=1,
    )
    chosen = jnp.concatenate(
        [
            lax.dynamic_slice_in_dim(energy, panel_order[k] * PANEL, PANEL, 0)
            for k in range(panel_order.shape[0])
        ]
    )
    window = panels.shape[1]
    width = total // n
    half, quarter = window // 2, window // 4
    dma = pltpu.SemaphoreType.DMA
    return pl.pallas_call(
        functools.partial(ring_kernel, n),
        out_shape=jax.ShapeDtypeStruct((depth, total), jnp.float32),
        in_specs=[pl.BlockSpec(memory_space=pltpu.VMEM)] * 4,
        out_specs=pl.BlockSpec(memory_space=pltpu.VMEM),
        scratch_shapes=[
            pltpu.VMEM((depth, total), jnp.float32),
            pltpu.VMEM((depth, half), jnp.float32),
            pltpu.VMEM((half, 2 * depth), jnp.bfloat16),
            pltpu.VMEM((half, 2 * depth), jnp.bfloat16),
            pltpu.VMEM((depth, window), jnp.bfloat16),
            pltpu.VMEM((depth, window), jnp.bfloat16),
            pltpu.VMEM((2, quarter, width), jnp.float32),
            pltpu.VMEM((2, n, quarter, width), jnp.float32),
            pltpu.VMEM((window, total), jnp.float32),
            dma, dma, dma((n,)), dma((n,)),
            dma((2, n - 1, SUB)), dma((2, n - 1, SUB)),
            dma((2, n - 1, SUB)), dma((2, n - 1, SUB)),
            dma((2, n, SUB)), dma((2, n, SUB)),
        ],
        compiler_params=pltpu.CompilerParams(
            collective_id=0, has_side_effects=True, vmem_limit_bytes=48 * 1024 * 1024
        ),
        cost_estimate=pl.CostEstimate(
            flops=12 * depth * window * total, bytes_accessed=8 * depth * total, transcendentals=0
        ),
    )(factors, panels, energy.reshape(1, total), chosen.reshape(window, 1))


def on_device(factors, occupied_energy, virtual_energy, batch_orbitals, panel_order):
    window = panel_order.shape[0] * PANEL
    fits = 4 * window * factors.shape[1] <= 8 * 1024 * 1024
    plan = by_rows if fits else by_columns
    return plan(factors, occupied_energy, virtual_energy, batch_orbitals, panel_order)


def solution(mesh):
    in_specs = (
        P(("groups", "pair", "aux"), None),
        P("groups"),
        P("groups"),
        P("groups"),
        P("groups"),
    )
    out_specs = P(("groups", "pair", "aux"), None)
    return jax.shard_map(
        on_device, mesh=mesh, in_specs=in_specs, out_specs=out_specs, check_vma=False
    )
```

```python
import functools

import jax
import jax.numpy as jnp
from jax import lax
from jax.experimental import pallas as pl
from jax.experimental.pallas import tpu as pltpu
from jax.sharding import PartitionSpec as P

PANEL = 64


os_scale = 1.3


def spread(block, axis, source):
    block = jnp.where(lax.axis_index(axis) == source, block, jnp.zeros_like(block))
    return lax.psum(block, axis)


def column_energies(columns, batch_energy, virtual_energy):
    nvir = virtual_energy.shape[0]
    nbatch = batch_energy.shape[0]
    orbital = columns // nvir
    virtual = columns % nvir
    occ_part = jnp.sum(
        jnp.where(
            orbital[:, None] == jnp.arange(nbatch, dtype=jnp.int32)[None, :],
            batch_energy[None, :],
            0.0,
        ),
        axis=1,
    )
    vir_part = jnp.sum(
        jnp.where(
            virtual[:, None] == jnp.arange(nvir, dtype=jnp.int32)[None, :],
            virtual_energy[None, :],
            0.0,
        ),
        axis=1,
    )
    return vir_part - occ_part


def batch_energies(occupied_energy, batch_orbitals):
    noccupied = occupied_energy.shape[0]
    return jnp.sum(
        jnp.where(
            batch_orbitals[:, None] == jnp.arange(noccupied, dtype=jnp.int32)[None, :],
            occupied_energy[None, :],
            0.0,
        ),
        axis=1,
    )


def by_columns(factors, occupied_energy, virtual_energy, batch_orbitals, panel_order):
    pair_count = lax.axis_size("pair")
    total_columns = factors.shape[1]
    col_local = total_columns // pair_count
    per_owner = col_local // PANEL
    working = lax.all_to_all(factors, "pair", split_axis=1, concat_axis=0, tiled=True)
    batch_energy = batch_energies(occupied_energy, batch_orbitals)
    own_columns = lax.axis_index("pair") * col_local + jnp.arange(col_local, dtype=jnp.int32)
    own_energy = column_energies(own_columns, batch_energy, virtual_energy)

    def one_panel(position, density):
        number = panel_order[position]
        owner_index = number // per_owner
        panel_slab = lax.dynamic_slice_in_dim(working, number % per_owner * PANEL, PANEL, 1)
        panel_block = spread(panel_slab, "pair", owner_index)
        panel_energy = column_energies(
            number * PANEL + jnp.arange(PANEL, dtype=jnp.int32), batch_energy, virtual_energy
        )
        partial_ints = lax.dot_general(
            panel_block,
            working,
            (((0,), (0,)), ((), ())),
            precision=lax.Precision.HIGHEST,
            preferred_element_type=jnp.float32,
        )
        integrals = lax.psum(partial_ints, "aux")
        amplitudes = os_scale * integrals / (own_energy[None, :] + panel_energy[:, None])
        return density + jnp.dot(
            panel_block,
            amplitudes,
            precision=lax.Precision.HIGHEST,
            preferred_element_type=jnp.float32,
        )

    density = lax.fori_loop(
        0, panel_order.shape[0], one_panel, jnp.zeros(working.shape, jnp.float32)
    )
    return lax.all_to_all(density, "pair", split_axis=0, concat_axis=1, tiled=True)


SUB = 2


def split(x):
    high = x.astype(jnp.bfloat16)
    return high, (x - high.astype(jnp.float32)).astype(jnp.bfloat16)


def dot3(a_high, a_low, b_high, b_low):
    dot = functools.partial(jnp.dot, preferred_element_type=jnp.float32)
    return dot(a_high, b_high) + dot(a_high, b_low) + dot(a_low, b_high)


def ring_place(pair, n):
    side = pair % 2
    level = pair // 2
    return level + side * (n - 1 - 2 * level)


def ring_pair(place, n):
    side = place // (n // 2)
    level = place + side * (n - 1 - 2 * place)
    return 2 * level + side


def panel_pair(ref, first, second):
    pair = 2 * PANEL

    def load(number):
        return ref[:, pl.ds(pl.multiple_of(number // 2 * pair, pair), pair)]

    left, right = load(first), load(second)
    left = jnp.where(first % 2 == 1, pltpu.roll(left, PANEL, 1), left)
    right = jnp.where(second % 2 == 0, pltpu.roll(right, PANEL, 1), right)
    lane = lax.broadcasted_iota(jnp.int32, left.shape, 1)
    return jnp.where(lane < PANEL, left, right)


def panel_kernel(
    order_ref, batch_ref, occupied_ref, virtual_ref, b_ref, p_ref, col_ref, row_ref
):
    nvir = virtual_ref.shape[1]
    for i in range(batch_ref.shape[0]):
        col_ref[:, i * nvir : (i + 1) * nvir] = virtual_ref[...] - occupied_ref[batch_ref[i]]
    pair = 2 * PANEL
    for k in range(order_ref.shape[0] // 2):
        first, second = order_ref[2 * k], order_ref[2 * k + 1]
        here = slice(k * pair, (k + 1) * pair)
        p_ref[:, here] = panel_pair(b_ref, first, second)
        chosen = panel_pair(col_ref, first, second)
        row_ref[here, :] = jnp.broadcast_to(chosen, (pair, pair)).T


def ring_kernel(
    n, b_ref, p_ref, col_ref, row_ref, out_ref,
    sib_b, sib_p, pt_high, pt_low, p_high, p_low, part, buf, amp,
    sibp_send, sibp_recv, sibb_send, sibb_recv,
    red_send, red_recv, gat_send, gat_recv, siba_send, siba_recv,
):
    depth, total = b_ref.shape
    window = p_ref.shape[1]
    width = total // n
    half = window // 2
    quarter = half // 2
    rows = quarter // SUB
    core = lax.axis_index("aux")
    place = ring_place(lax.axis_index("pair"), n)

    def neighbour(d):
        return {"pair": ring_pair((place + n + 1 - 2 * d) % n, n)}

    sibling = {"aux": 1 - core}

    def columns(q):
        return pl.ds(pl.multiple_of(q * width, width), width)

    def shard(d, step):
        return (place + n * n + (2 * d - 1) * step) % n

    def sib_p_copy():
        return pltpu.make_async_remote_copy(
            p_ref.at[:, pl.ds(pl.multiple_of((1 - core) * half, half), half)], sib_p,
            sibp_send, sibp_recv, device_id=sibling, device_id_type=pl.DeviceIdType.MESH)

    def sib_b_copy(q):
        return pltpu.make_async_remote_copy(
            b_ref.at[:, columns(q)], sib_b.at[:, columns(q)],
            sibb_send.at[q], sibb_recv.at[q], device_id=sibling,
            device_id_type=pl.DeviceIdType.MESH)

    def sub(u):
        return pl.ds(pl.multiple_of(u * rows, rows), rows)

    def amp_rows(d, u):
        return pl.ds(pl.multiple_of(core * half + d * quarter + u * rows, rows), rows)

    def red_copy(d, s, u):
        return pltpu.make_async_remote_copy(
            buf.at[d, s, sub(u)], buf.at[d, s + 1, sub(u)],
            red_send.at[d, s, u], red_recv.at[d, s, u], device_id=neighbour(d),
            device_id_type=pl.DeviceIdType.MESH)

    def gat_copy(d, s, u, q):
        block = amp.at[amp_rows(d, u), columns(q)]
        return pltpu.make_async_remote_copy(
            block, block, gat_send.at[d, s, u], gat_recv.at[d, s, u],
            device_id=neighbour(d), device_id_type=pl.DeviceIdType.MESH)

    def sib_a_copy(d, t, u, q):
        block = amp.at[amp_rows(d, u), columns(q)]
        return pltpu.make_async_remote_copy(
            block, block, siba_send.at[d, t, u], siba_recv.at[d, t, u],
            device_id=sibling, device_id_type=pl.DeviceIdType.MESH)

    def sib_a_arrival(d, t, u, q):
        block = amp.at[
            pl.ds(pl.multiple_of((1 - core) * half + d * quarter + u * rows, rows), rows),
            columns(q)]
        return pltpu.make_async_remote_copy(
            block, block, siba_send.at[d, t, u], siba_recv.at[d, t, u],
            device_id=sibling, device_id_type=pl.DeviceIdType.MESH)

    barrier = pltpu.get_barrier_semaphore()
    for other in (neighbour(0), neighbour(1), sibling):
        pl.semaphore_signal(barrier, inc=1, device_id=other, device_id_type=pl.DeviceIdType.MESH)
    pl.semaphore_wait(barrier, 3)

    sib_p_copy().start()
    for i in range(1, n // 2 + 1):
        sib_b_copy(shard(0, i)).start()
        if i < n // 2:
            sib_b_copy(shard(1, i)).start()
    sib_b_copy(place).start()

    mine = pl.ds(pl.multiple_of(core * half, half), half)
    high, low = split(p_ref[:, mine].T)
    pt_high[:, :depth] = high
    pt_low[:, :depth] = low
    sib_p_copy().wait_recv()
    high, low = split(sib_p[...].T)
    pt_high[:, depth:] = high
    pt_low[:, depth:] = low

    def set_part(d, q):
        lhs = pl.ds(pl.multiple_of(d * quarter, quarter), quarter)
        own_high, own_low = split(b_ref[:, columns(q)])
        sib_high, sib_low = split(sib_b[:, columns(q)])
        part[d] = dot3(pt_high[lhs, :depth], pt_low[lhs, :depth], own_high, own_low) + dot3(
            pt_high[lhs, depth:], pt_low[lhs, depth:], sib_high, sib_low)

    @pl.loop(0, 2)
    def _(d):
        sib_b_copy(shard(d, 1)).wait_recv()
        set_part(d, shard(d, 1))
        buf[d, 0] = part[d]
        for u in range(SUB):
            red_copy(d, 0, u).start()

    for i in range(2, n // 2 + 1):
        sib_b_copy(shard(0, i)).wait_recv()
        if i < n // 2:
            sib_b_copy(shard(1, i)).wait_recv()
    sib_b_copy(place).wait_recv()
    high, low = split(p_ref[...])
    p_high[...] = high
    p_low[...] = low

    @pl.loop(1, n - 1)
    def _(s):
        @pl.loop(0, 2)
        def _(d):
            set_part(d, shard(d, s + 1))
        for u in range(SUB):
            for d in range(2):
                red_copy(d, s - 1, u).wait_recv()
                buf[d, s, sub(u)] += part[d, sub(u)]
                red_copy(d, s, u).start()

    @pl.loop(0, 2)
    def _(d):
        set_part(d, place)
    for u in range(SUB):
        for d in range(2):
            red_copy(d, n - 2, u).wait_recv()
            integrals = buf[d, n - 1, sub(u)] + part[d, sub(u)]
            energy = col_ref[:, columns(place)] + row_ref[amp_rows(d, u), 0:1]
            amp[amp_rows(d, u), columns(place)] = os_scale * integrals / energy
            gat_copy(d, 0, u, place).start()
            sib_a_copy(d, 0, u, place).start()

    def pass_on(s, last):
        for u in range(SUB):
            for d in range(2):
                q = shard(d, s + 1)
                gat_copy(d, s, u, q).wait_recv()
                if not last:
                    gat_copy(d, s + 1, u, q).start()
                sib_a_copy(d, s + 1, u, q).start()

    def density(q):
        total_sum = jnp.zeros((depth, width), jnp.float32)
        for k in range(4):
            span = pl.ds(k * quarter, quarter)
            a_high, a_low = split(amp[span, columns(q)])
            total_sum += dot3(p_high[:, span], p_low[:, span], a_high, a_low)
        out_ref[:, columns(q)] = total_sum

    def finish(d, j):
        q = shard(d, j)
        for u in range(SUB):
            sib_a_arrival(d, j, u, q).wait_recv()
            sib_a_arrival(1 - d, (n - j) % n, u, q).wait_recv()
        density(q)

    middle = n // 2

    @pl.loop(0, middle)
    def _(s):
        pass_on(s, False)

    @pl.loop(0, 2)
    def _(i):
        finish(0, i * middle)

    @pl.loop(middle, n - 2)
    def _(s):
        pass_on(s, False)

        @pl.loop(0, 2)
        def _(d):
            finish(d, n - 1 - s)

    pass_on(n - 2, True)

    @pl.loop(0, 2)
    def _(d):
        finish(d, 1)

    sib_p_copy().wait_send()

    @pl.loop(0, n)
    def _(q):
        sib_b_copy(q).wait_send()

    for d in range(2):
        for u in range(SUB):
            @pl.loop(0, n - 1)
            def _(s):
                red_copy(d, s, u).wait_send()
                gat_copy(d, s, u, shard(d, s)).wait_send()

            @pl.loop(0, n)
            def _(t):
                sib_a_copy(d, t, u, shard(d, t)).wait_send()


def by_rows(factors, occupied_energy, virtual_energy, batch_orbitals, panel_order):
    n = lax.axis_size("pair")
    depth, total = factors.shape
    window = panel_order.shape[0] * PANEL
    width = total // n
    half, quarter = window // 2, window // 4
    dma = pltpu.SemaphoreType.DMA
    panels, energy, chosen = pl.pallas_call(
        panel_kernel,
        out_shape=[
            jax.ShapeDtypeStruct((depth, window), jnp.float32),
            jax.ShapeDtypeStruct((1, total), jnp.float32),
            jax.ShapeDtypeStruct((window, 2 * PANEL), jnp.float32),
        ],
        in_specs=[pl.BlockSpec(memory_space=pltpu.SMEM)] * 3
        + [pl.BlockSpec(memory_space=pltpu.VMEM)] * 2,
        out_specs=[pl.BlockSpec(memory_space=pltpu.VMEM)] * 3,
    )(panel_order, batch_orbitals, occupied_energy, virtual_energy.reshape(1, -1), factors)
    return pl.pallas_call(
        functools.partial(ring_kernel, n),
        out_shape=jax.ShapeDtypeStruct((depth, total), jnp.float32),
        in_specs=[pl.BlockSpec(memory_space=pltpu.VMEM)] * 4,
        out_specs=pl.BlockSpec(memory_space=pltpu.VMEM),
        scratch_shapes=[
            pltpu.VMEM((depth, total), jnp.float32),
            pltpu.VMEM((depth, half), jnp.float32),
            pltpu.VMEM((half, 2 * depth), jnp.bfloat16),
            pltpu.VMEM((half, 2 * depth), jnp.bfloat16),
            pltpu.VMEM((depth, window), jnp.bfloat16),
            pltpu.VMEM((depth, window), jnp.bfloat16),
            pltpu.VMEM((2, quarter, width), jnp.float32),
            pltpu.VMEM((2, n, quarter, width), jnp.float32),
            pltpu.VMEM((window, total), jnp.float32),
            dma, dma, dma((n,)), dma((n,)),
            dma((2, n - 1, SUB)), dma((2, n - 1, SUB)),
            dma((2, n - 1, SUB)), dma((2, n - 1, SUB)),
            dma((2, n, SUB)), dma((2, n, SUB)),
        ],
        compiler_params=pltpu.CompilerParams(
            collective_id=0, has_side_effects=True, vmem_limit_bytes=48 * 1024 * 1024
        ),
        cost_estimate=pl.CostEstimate(
            flops=12 * depth * window * total, bytes_accessed=8 * depth * total, transcendentals=0
        ),
    )(factors, panels, energy, chosen)


def on_device(factors, occupied_energy, virtual_energy, batch_orbitals, panel_order):
    window = panel_order.shape[0] * PANEL
    fits = 4 * window * factors.shape[1] <= 8 * 1024 * 1024
    plan = by_rows if fits else by_columns
    return plan(factors, occupied_energy, virtual_energy, batch_orbitals, panel_order)


def solution(mesh):
    in_specs = (
        P(("groups", "pair", "aux"), None),
        P("groups"),
        P("groups"),
        P("groups"),
        P("groups"),
    )
    out_specs = P(("groups", "pair", "aux"), None)
    return jax.shard_map(
        on_device, mesh=mesh, in_specs=in_specs, out_specs=out_specs, check_vma=False
    )
```

```python
import functools

import jax
import jax.numpy as jnp
from jax import lax
from jax.experimental import pallas as pl
from jax.experimental.pallas import tpu as pltpu
from jax.sharding import PartitionSpec as P

PANEL = 64


os_scale = 1.3


def spread(block, axis, source):
    block = jnp.where(lax.axis_index(axis) == source, block, jnp.zeros_like(block))
    return lax.psum(block, axis)


def column_energies(columns, batch_energy, virtual_energy):
    nvir = virtual_energy.shape[0]
    nbatch = batch_energy.shape[0]
    orbital = columns // nvir
    virtual = columns % nvir
    occ_part = jnp.sum(
        jnp.where(
            orbital[:, None] == jnp.arange(nbatch, dtype=jnp.int32)[None, :],
            batch_energy[None, :],
            0.0,
        ),
        axis=1,
    )
    vir_part = jnp.sum(
        jnp.where(
            virtual[:, None] == jnp.arange(nvir, dtype=jnp.int32)[None, :],
            virtual_energy[None, :],
            0.0,
        ),
        axis=1,
    )
    return vir_part - occ_part


def batch_energies(occupied_energy, batch_orbitals):
    noccupied = occupied_energy.shape[0]
    return jnp.sum(
        jnp.where(
            batch_orbitals[:, None] == jnp.arange(noccupied, dtype=jnp.int32)[None, :],
            occupied_energy[None, :],
            0.0,
        ),
        axis=1,
    )


def by_columns(factors, occupied_energy, virtual_energy, batch_orbitals, panel_order):
    pair_count = lax.axis_size("pair")
    total_columns = factors.shape[1]
    col_local = total_columns // pair_count
    per_owner = col_local // PANEL
    working = lax.all_to_all(factors, "pair", split_axis=1, concat_axis=0, tiled=True)
    batch_energy = batch_energies(occupied_energy, batch_orbitals)
    own_columns = lax.axis_index("pair") * col_local + jnp.arange(col_local, dtype=jnp.int32)
    own_energy = column_energies(own_columns, batch_energy, virtual_energy)

    def one_panel(position, density):
        number = panel_order[position]
        owner_index = number // per_owner
        panel_slab = lax.dynamic_slice_in_dim(working, number % per_owner * PANEL, PANEL, 1)
        panel_block = spread(panel_slab, "pair", owner_index)
        panel_energy = column_energies(
            number * PANEL + jnp.arange(PANEL, dtype=jnp.int32), batch_energy, virtual_energy
        )
        partial_ints = lax.dot_general(
            panel_block,
            working,
            (((0,), (0,)), ((), ())),
            precision=lax.Precision.HIGHEST,
            preferred_element_type=jnp.float32,
        )
        integrals = lax.psum(partial_ints, "aux")
        amplitudes = os_scale * integrals / (own_energy[None, :] + panel_energy[:, None])
        return density + jnp.dot(
            panel_block,
            amplitudes,
            precision=lax.Precision.HIGHEST,
            preferred_element_type=jnp.float32,
        )

    density = lax.fori_loop(
        0, panel_order.shape[0], one_panel, jnp.zeros(working.shape, jnp.float32)
    )
    return lax.all_to_all(density, "pair", split_axis=0, concat_axis=1, tiled=True)


SUB = 2


def split(x):
    high = x.astype(jnp.bfloat16)
    return high, (x - high.astype(jnp.float32)).astype(jnp.bfloat16)


def dot3(a_high, a_low, b_high, b_low):
    dot = functools.partial(jnp.dot, preferred_element_type=jnp.float32)
    return dot(a_high, b_high) + dot(a_high, b_low) + dot(a_low, b_high)


def ring_place(pair, n):
    side = pair % 2
    level = pair // 2
    return level + side * (n - 1 - 2 * level)


def ring_pair(place, n):
    side = place // (n // 2)
    level = place + side * (n - 1 - 2 * place)
    return 2 * level + side


def panel_pair(ref, first, second):
    pair = 2 * PANEL

    def load(number):
        return ref[:, pl.ds(pl.multiple_of(number // 2 * pair, pair), pair)]

    left, right = load(first), load(second)
    left = jnp.where(first % 2 == 1, pltpu.roll(left, PANEL, 1), left)
    right = jnp.where(second % 2 == 0, pltpu.roll(right, PANEL, 1), right)
    lane = lax.broadcasted_iota(jnp.int32, left.shape, 1)
    return jnp.where(lane < PANEL, left, right)


def sort_kernel(
    order_ref, batch_ref, occupied_ref, virtual_ref, b_ref,
    place_ref, b_out, col_out, row_out, source, energy,
):
    nvir = virtual_ref.shape[1]
    for i in range(batch_ref.shape[0]):
        energy[:, i * nvir : (i + 1) * nvir] = virtual_ref[...] - occupied_ref[batch_ref[i]]
    listed, panels = order_ref.shape[0], place_ref.shape[0]
    for j in range(panels):
        place_ref[j] = -1
    for k in range(listed):
        place_ref[order_ref[k]] = k
        source[k] = order_ref[k]
    free = jnp.int32(listed)
    for j in range(panels):
        found = place_ref[j]
        source[free] = j
        place_ref[j] = jnp.where(found < 0, free, found)
        free = jnp.where(found < 0, free + 1, free)
    pair = 2 * PANEL
    window = listed * PANEL
    for k in range(panels // 2):
        first, second = source[2 * k], source[2 * k + 1]
        here = slice(k * pair, (k + 1) * pair)
        b_out[:, here] = panel_pair(b_ref, first, second)
        chosen = panel_pair(energy, first, second)
        col_out[:, here] = chosen
        if k < listed // 2:
            row_out[here, :] = jnp.broadcast_to(chosen, (pair, pair)).T
    row_out[window:, :] = row_out[: row_out.shape[0] - window, :]


def unsort_kernel(place_ref, d_ref, out_ref):
    pair = 2 * PANEL
    for k in range(place_ref.shape[0] // 2):
        here = slice(k * pair, (k + 1) * pair)
        out_ref[:, here] = panel_pair(d_ref, place_ref[2 * k], place_ref[2 * k + 1])


def ring_kernel(
    n, b_ref, col_ref, row_ref, out_ref,
    sib_b, pt_high, pt_low, p_high, p_low, energy, part, buf, amp,
    sibp_send, sibp_recv, sibb_send, sibb_recv,
    red_send, red_recv, gat_send, gat_recv, siba_send, siba_recv,
):
    depth, total = b_ref.shape
    window = total // 2
    width = window // n
    near = (n // 2 + 1) * width
    near_rows, far_rows = near // 4, window // 4
    rows = (near_rows + far_rows) // SUB
    core = lax.axis_index("aux")
    place = ring_place(lax.axis_index("pair"), n)

    def neighbour(d):
        return {"pair": ring_pair((place + n + 1 - 2 * d) % n, n)}

    sibling = {"aux": 1 - core}

    def columns(q):
        return pl.ds(pl.multiple_of(q * width, width), width)

    def far_columns(q):
        return pl.ds(pl.multiple_of(window + q * width, width), width)

    def near_span(d, q):
        return pl.ds(pl.multiple_of(q * width + (2 * core + d) * near_rows, 32), near_rows)

    def far_span(d):
        return pl.ds(pl.multiple_of((2 * core + d) * far_rows, 32), far_rows)

    def shard(d, step):
        return (place + n * n + (2 * d - 1) * step) % n

    def sib_p_copy():
        return pltpu.make_async_remote_copy(
            b_ref.at[:, pl.ds(0, window)], sib_b.at[:, pl.ds(0, window)],
            sibp_send, sibp_recv, device_id=sibling, device_id_type=pl.DeviceIdType.MESH)

    def sib_b_copy(q):
        return pltpu.make_async_remote_copy(
            b_ref.at[:, far_columns(q)], sib_b.at[:, far_columns(q)],
            sibb_send.at[q], sibb_recv.at[q], device_id=sibling,
            device_id_type=pl.DeviceIdType.MESH)

    def sub(u):
        return pl.ds(pl.multiple_of(u * rows, rows), rows)

    def red_copy(d, s, u):
        return pltpu.make_async_remote_copy(
            buf.at[d, s, sub(u)], buf.at[d, s + 1, sub(u)],
            red_send.at[d, s, u], red_recv.at[d, s, u], device_id=neighbour(d),
            device_id_type=pl.DeviceIdType.MESH)

    def gat_copy(d, s, u, q):
        block = amp.at[q, core, d, sub(u)]
        return pltpu.make_async_remote_copy(
            block, block, gat_send.at[d, s, u], gat_recv.at[d, s, u],
            device_id=neighbour(d), device_id_type=pl.DeviceIdType.MESH)

    def sib_a_copy(d, t, u, q):
        block = amp.at[q, core, d, sub(u)]
        return pltpu.make_async_remote_copy(
            block, block, siba_send.at[d, t, u], siba_recv.at[d, t, u],
            device_id=sibling, device_id_type=pl.DeviceIdType.MESH)

    def sib_a_arrival(d, t, u, q):
        block = amp.at[q, 1 - core, d, sub(u)]
        return pltpu.make_async_remote_copy(
            block, block, siba_send.at[d, t, u], siba_recv.at[d, t, u],
            device_id=sibling, device_id_type=pl.DeviceIdType.MESH)

    barrier = pltpu.get_barrier_semaphore()
    for other in (neighbour(0), neighbour(1), sibling):
        pl.semaphore_signal(barrier, inc=1, device_id=other, device_id_type=pl.DeviceIdType.MESH)
    pl.semaphore_wait(barrier, 3)

    sib_p_copy().start()
    for i in range(1, n // 2 + 1):
        sib_b_copy(shard(0, i)).start()
        if i < n // 2:
            sib_b_copy(shard(1, i)).start()
    sib_b_copy(place).start()

    def set_transposed(ref, span):
        high, low = split(ref[:, :window].T)
        pt_high[:window, span] = high
        pt_low[:window, span] = low
        pt_high[window:, span] = high[:near]
        pt_low[window:, span] = low[:near]

    set_transposed(b_ref, slice(0, depth))
    sib_p_copy().wait_recv()
    set_transposed(sib_b, slice(depth, 2 * depth))

    def set_part(d, q):
        def product(lhs, cols):
            both = jnp.concatenate([b_ref[:, cols], sib_b[:, cols]], axis=0)
            return dot3(pt_high[lhs, :], pt_low[lhs, :], *split(both))

        part[d, :near_rows] = product(near_span(d, q), columns(q))
        part[d, near_rows:] = product(far_span(d), far_columns(q))

    @pl.loop(0, 2)
    def _(d):
        sib_b_copy(shard(d, 1)).wait_recv()
        set_part(d, shard(d, 1))
        buf[d, 0] = part[d]
        for u in range(SUB):
            red_copy(d, 0, u).start()

    for i in range(2, n // 2 + 1):
        sib_b_copy(shard(0, i)).wait_recv()
        if i < n // 2:
            sib_b_copy(shard(1, i)).wait_recv()
    sib_b_copy(place).wait_recv()
    high, low = split(b_ref[:, :window])
    p_high[:, :window] = high
    p_low[:, :window] = low
    p_high[:, window:] = high[:, :near]
    p_low[:, window:] = low[:, :near]
    out_ref[:, :window] = jnp.zeros((depth, window), jnp.float32)
    for d in range(2):
        energy[d, :near_rows] = row_ref[near_span(d, place), :] + col_ref[:, columns(place)]
        energy[d, near_rows:] = row_ref[far_span(d), :] + col_ref[:, far_columns(place)]

    @pl.loop(1, n - 1)
    def _(s):
        @pl.loop(0, 2)
        def _(d):
            set_part(d, shard(d, s + 1))
        for u in range(SUB):
            for d in range(2):
                red_copy(d, s - 1, u).wait_recv()
                buf[d, s, sub(u)] += part[d, sub(u)]
                red_copy(d, s, u).start()

    @pl.loop(0, 2)
    def _(d):
        set_part(d, place)
    for u in range(SUB):
        for d in range(2):
            red_copy(d, n - 2, u).wait_recv()
            integrals = buf[d, n - 1, sub(u)] + part[d, sub(u)]
            amp[place, core, d, sub(u)] = os_scale * integrals / energy[d, sub(u)]
            gat_copy(d, 0, u, place).start()
            sib_a_copy(d, 0, u, place).start()

    def pass_on(s, last):
        for u in range(SUB):
            for d in range(2):
                q = shard(d, s + 1)
                gat_copy(d, s, u, q).wait_recv()
                if not last:
                    gat_copy(d, s + 1, u, q).start()
                sib_a_copy(d, s + 1, u, q).start()

    def density(q):
        far = jnp.zeros((depth, width), jnp.float32)
        for j in range(4):
            span = slice(j * far_rows, (j + 1) * far_rows)
            far += dot3(
                p_high[:, span], p_low[:, span], *split(amp[q, j // 2, j % 2, near_rows:]))
        out_ref[:, far_columns(q)] = far
        block = jnp.concatenate([amp[q, j // 2, j % 2, :near_rows] for j in range(4)], axis=0)
        high, low = split(block)
        span = pl.ds(pl.multiple_of(q * width, width), near)
        out_ref[:, columns(q)] += dot3(p_high[:, span], p_low[:, span], high, low)
        q_high, q_low = p_high[:, columns(q)], p_low[:, columns(q)]
        for i in range(1, n // 2):
            there = slice(i * width, (i + 1) * width)
            out_ref[:, columns((q + i) % n)] += dot3(
                q_high, q_low, high[there].T, low[there].T)

    def finish(d, j):
        q = shard(d, j)
        for u in range(SUB):
            sib_a_arrival(d, j, u, q).wait_recv()
            sib_a_arrival(1 - d, (n - j) % n, u, q).wait_recv()
        density(q)

    middle = n // 2

    @pl.loop(0, middle)
    def _(s):
        pass_on(s, False)

    @pl.loop(0, 2)
    def _(i):
        finish(0, i * middle)

    @pl.loop(middle, n - 2)
    def _(s):
        pass_on(s, False)

        @pl.loop(0, 2)
        def _(d):
            finish(d, n - 1 - s)

    pass_on(n - 2, True)

    @pl.loop(0, 2)
    def _(d):
        finish(d, 1)

    sib_p_copy().wait_send()

    @pl.loop(0, n)
    def _(q):
        sib_b_copy(q).wait_send()

    for d in range(2):
        for u in range(SUB):
            @pl.loop(0, n - 1)
            def _(s):
                red_copy(d, s, u).wait_send()
                gat_copy(d, s, u, shard(d, s)).wait_send()

            @pl.loop(0, n)
            def _(t):
                sib_a_copy(d, t, u, shard(d, t)).wait_send()


def by_rows(factors, occupied_energy, virtual_energy, batch_orbitals, panel_order):
    n = lax.axis_size("pair")
    depth, total = factors.shape
    window = panel_order.shape[0] * PANEL
    width = window // n
    near = (n // 2 + 1) * width
    stream = (near + window) // 4
    dma = pltpu.SemaphoreType.DMA
    smem, vmem = pl.BlockSpec(memory_space=pltpu.SMEM), pl.BlockSpec(memory_space=pltpu.VMEM)
    place, ordered, energy, rows = pl.pallas_call(
        sort_kernel,
        out_shape=[
            jax.ShapeDtypeStruct((total // PANEL,), jnp.int32),
            jax.ShapeDtypeStruct((depth, total), jnp.float32),
            jax.ShapeDtypeStruct((1, total), jnp.float32),
            jax.ShapeDtypeStruct((window + near, 2 * PANEL), jnp.float32),
        ],
        in_specs=[smem] * 3 + [vmem] * 2,
        out_specs=[smem] + [vmem] * 3,
        scratch_shapes=[
            pltpu.SMEM((total // PANEL + 1,), jnp.int32),
            pltpu.VMEM((1, total), jnp.float32),
        ],
    )(panel_order, batch_orbitals, occupied_energy, virtual_energy.reshape(1, -1), factors)
    density = pl.pallas_call(
        functools.partial(ring_kernel, n),
        out_shape=jax.ShapeDtypeStruct((depth, total), jnp.float32),
        in_specs=[vmem] * 3,
        out_specs=vmem,
        scratch_shapes=[
            pltpu.VMEM((depth, total), jnp.float32),
            pltpu.VMEM((window + near, 2 * depth), jnp.bfloat16),
            pltpu.VMEM((window + near, 2 * depth), jnp.bfloat16),
            pltpu.VMEM((depth, window + near), jnp.bfloat16),
            pltpu.VMEM((depth, window + near), jnp.bfloat16),
            pltpu.VMEM((2, stream, width), jnp.float32),
            pltpu.VMEM((2, stream, width), jnp.float32),
            pltpu.VMEM((2, n, stream, width), jnp.float32),
            pltpu.VMEM((n, 2, 2, stream, width), jnp.float32),
            dma, dma, dma((n,)), dma((n,)),
            dma((2, n - 1, SUB)), dma((2, n - 1, SUB)),
            dma((2, n - 1, SUB)), dma((2, n - 1, SUB)),
            dma((2, n, SUB)), dma((2, n, SUB)),
        ],
        compiler_params=pltpu.CompilerParams(
            collective_id=0, has_side_effects=True, vmem_limit_bytes=48 * 1024 * 1024
        ),
        cost_estimate=pl.CostEstimate(
            flops=12 * depth * window * total, bytes_accessed=8 * depth * total, transcendentals=0
        ),
    )(ordered, energy, rows)
    return pl.pallas_call(
        unsort_kernel,
        out_shape=jax.ShapeDtypeStruct((depth, total), jnp.float32),
        in_specs=[smem, vmem],
        out_specs=vmem,
    )(place, density)


def on_device(factors, occupied_energy, virtual_energy, batch_orbitals, panel_order):
    window = panel_order.shape[0] * PANEL
    n = lax.axis_size("pair")
    fits = n % 2 == 0 and window == 2 * PANEL * n and factors.shape[1] == 2 * window
    plan = by_rows if fits else by_columns
    return plan(factors, occupied_energy, virtual_energy, batch_orbitals, panel_order)


def solution(mesh):
    in_specs = (
        P(("groups", "pair", "aux"), None),
        P("groups"),
        P("groups"),
        P("groups"),
        P("groups"),
    )
    out_specs = P(("groups", "pair", "aux"), None)
    return jax.shard_map(
        on_device, mesh=mesh, in_specs=in_specs, out_specs=out_specs, check_vma=False
    )
```

```python
import functools

import jax
import jax.numpy as jnp
from jax import lax
from jax.experimental import pallas as pl
from jax.experimental.pallas import tpu as pltpu
from jax.sharding import PartitionSpec as P

PANEL = 64


os_scale = 1.3


def spread(block, axis, source):
    block = jnp.where(lax.axis_index(axis) == source, block, jnp.zeros_like(block))
    return lax.psum(block, axis)


def column_energies(columns, batch_energy, virtual_energy):
    nvir = virtual_energy.shape[0]
    nbatch = batch_energy.shape[0]
    orbital = columns // nvir
    virtual = columns % nvir
    occ_part = jnp.sum(
        jnp.where(
            orbital[:, None] == jnp.arange(nbatch, dtype=jnp.int32)[None, :],
            batch_energy[None, :],
            0.0,
        ),
        axis=1,
    )
    vir_part = jnp.sum(
        jnp.where(
            virtual[:, None] == jnp.arange(nvir, dtype=jnp.int32)[None, :],
            virtual_energy[None, :],
            0.0,
        ),
        axis=1,
    )
    return vir_part - occ_part


def batch_energies(occupied_energy, batch_orbitals):
    noccupied = occupied_energy.shape[0]
    return jnp.sum(
        jnp.where(
            batch_orbitals[:, None] == jnp.arange(noccupied, dtype=jnp.int32)[None, :],
            occupied_energy[None, :],
            0.0,
        ),
        axis=1,
    )


def by_columns(factors, occupied_energy, virtual_energy, batch_orbitals, panel_order):
    pair_count = lax.axis_size("pair")
    total_columns = factors.shape[1]
    col_local = total_columns // pair_count
    per_owner = col_local // PANEL
    working = lax.all_to_all(factors, "pair", split_axis=1, concat_axis=0, tiled=True)
    batch_energy = batch_energies(occupied_energy, batch_orbitals)
    own_columns = lax.axis_index("pair") * col_local + jnp.arange(col_local, dtype=jnp.int32)
    own_energy = column_energies(own_columns, batch_energy, virtual_energy)

    def one_panel(position, density):
        number = panel_order[position]
        owner_index = number // per_owner
        panel_slab = lax.dynamic_slice_in_dim(working, number % per_owner * PANEL, PANEL, 1)
        panel_block = spread(panel_slab, "pair", owner_index)
        panel_energy = column_energies(
            number * PANEL + jnp.arange(PANEL, dtype=jnp.int32), batch_energy, virtual_energy
        )
        partial_ints = lax.dot_general(
            panel_block,
            working,
            (((0,), (0,)), ((), ())),
            precision=lax.Precision.HIGHEST,
            preferred_element_type=jnp.float32,
        )
        integrals = lax.psum(partial_ints, "aux")
        amplitudes = os_scale * integrals / (own_energy[None, :] + panel_energy[:, None])
        return density + jnp.dot(
            panel_block,
            amplitudes,
            precision=lax.Precision.HIGHEST,
            preferred_element_type=jnp.float32,
        )

    density = lax.fori_loop(
        0, panel_order.shape[0], one_panel, jnp.zeros(working.shape, jnp.float32)
    )
    return lax.all_to_all(density, "pair", split_axis=0, concat_axis=1, tiled=True)


SUB = 2


def split(x):
    high = x.astype(jnp.bfloat16)
    return high, (x - high.astype(jnp.float32)).astype(jnp.bfloat16)


def dot3(a_high, a_low, b_high, b_low):
    dot = functools.partial(jnp.dot, preferred_element_type=jnp.float32)
    return dot(a_high, b_high) + dot(a_high, b_low) + dot(a_low, b_high)


def ring_place(pair, n):
    side = pair % 2
    level = pair // 2
    return level + side * (n - 1 - 2 * level)


def ring_pair(place, n):
    side = place // (n // 2)
    level = place + side * (n - 1 - 2 * place)
    return 2 * level + side


def panel_pair(ref, first, second):
    pair = 2 * PANEL

    def load(number):
        return ref[:, pl.ds(pl.multiple_of(number // 2 * pair, pair), pair)]

    left, right = load(first), load(second)
    left = jnp.where(first % 2 == 1, pltpu.roll(left, PANEL, 1), left)
    right = jnp.where(second % 2 == 0, pltpu.roll(right, PANEL, 1), right)
    lane = lax.broadcasted_iota(jnp.int32, left.shape, 1)
    return jnp.where(lane < PANEL, left, right)


def sort_kernel(
    order_ref, batch_ref, occupied_ref, virtual_ref, b_ref,
    place_ref, b_out, source, energy,
):
    depth = b_ref.shape[0]
    nvir = virtual_ref.shape[1]
    for i in range(batch_ref.shape[0]):
        energy[:, i * nvir : (i + 1) * nvir] = virtual_ref[...] - occupied_ref[batch_ref[i]]
    listed, panels = order_ref.shape[0], place_ref.shape[0]
    for j in range(panels):
        place_ref[j] = -1
    for k in range(listed):
        place_ref[order_ref[k]] = k
        source[k] = order_ref[k]
    free = jnp.int32(listed)
    for j in range(panels):
        found = place_ref[j]
        source[free] = j
        place_ref[j] = jnp.where(found < 0, free, found)
        free = jnp.where(found < 0, free + 1, free)
    pair = 2 * PANEL
    for k in range(panels // 2):
        first, second = source[2 * k], source[2 * k + 1]
        here = slice(k * pair, (k + 1) * pair)
        b_out[:depth, here] = panel_pair(b_ref, first, second)
        b_out[depth:, here] = jnp.broadcast_to(panel_pair(energy, first, second), (8, pair))


def unsort_kernel(place_ref, d_ref, out_ref):
    pair = 2 * PANEL
    for k in range(place_ref.shape[0] // 2):
        here = slice(k * pair, (k + 1) * pair)
        out_ref[:, here] = panel_pair(d_ref, place_ref[2 * k], place_ref[2 * k + 1])


def ring_kernel(
    n, b_ref, out_ref,
    row_ref, sib_b, pt_high, pt_low, p_high, p_low, energy, part, buf, amp,
    sibp_send, sibp_recv, sibb_send, sibb_recv,
    red_send, red_recv, gat_send, gat_recv, siba_send, siba_recv,
):
    depth, total = out_ref.shape
    window = total // 2
    width = window // n
    near = (n // 2 + 1) * width
    near_rows, far_rows = near // 4, window // 4
    rows = (near_rows + far_rows) // SUB
    core = lax.axis_index("aux")
    place = ring_place(lax.axis_index("pair"), n)

    def neighbour(d):
        return {"pair": ring_pair((place + n + 1 - 2 * d) % n, n)}

    sibling = {"aux": 1 - core}

    def columns(q):
        return pl.ds(pl.multiple_of(q * width, width), width)

    def far_columns(q):
        return pl.ds(pl.multiple_of(window + q * width, width), width)

    def near_span(d, q):
        return pl.ds(pl.multiple_of(q * width + (2 * core + d) * near_rows, 32), near_rows)

    def far_span(d):
        return pl.ds(pl.multiple_of((2 * core + d) * far_rows, 32), far_rows)

    def shard(d, step):
        return (place + n * n + (2 * d - 1) * step) % n

    def sib_p_copy():
        return pltpu.make_async_remote_copy(
            b_ref.at[pl.ds(0, depth), pl.ds(0, window)], sib_b.at[:, pl.ds(0, window)],
            sibp_send, sibp_recv, device_id=sibling, device_id_type=pl.DeviceIdType.MESH)

    def sib_b_copy(q):
        return pltpu.make_async_remote_copy(
            b_ref.at[pl.ds(0, depth), far_columns(q)], sib_b.at[:, far_columns(q)],
            sibb_send.at[q], sibb_recv.at[q], device_id=sibling,
            device_id_type=pl.DeviceIdType.MESH)

    def sub(u):
        return pl.ds(pl.multiple_of(u * rows, rows), rows)

    def red_copy(d, s, u):
        return pltpu.make_async_remote_copy(
            buf.at[d, s, sub(u)], buf.at[d, s + 1, sub(u)],
            red_send.at[d, s, u], red_recv.at[d, s, u], device_id=neighbour(d),
            device_id_type=pl.DeviceIdType.MESH)

    def gat_copy(d, s, u, q):
        block = amp.at[q, core, d, sub(u)]
        return pltpu.make_async_remote_copy(
            block, block, gat_send.at[d, s, u], gat_recv.at[d, s, u],
            device_id=neighbour(d), device_id_type=pl.DeviceIdType.MESH)

    def sib_a_copy(d, t, u, q):
        block = amp.at[q, core, d, sub(u)]
        return pltpu.make_async_remote_copy(
            block, block, siba_send.at[d, t, u], siba_recv.at[d, t, u],
            device_id=sibling, device_id_type=pl.DeviceIdType.MESH)

    def sib_a_arrival(d, t, u, q):
        block = amp.at[q, 1 - core, d, sub(u)]
        return pltpu.make_async_remote_copy(
            block, block, siba_send.at[d, t, u], siba_recv.at[d, t, u],
            device_id=sibling, device_id_type=pl.DeviceIdType.MESH)

    barrier = pltpu.get_barrier_semaphore()
    for other in (neighbour(0), neighbour(1), sibling):
        pl.semaphore_signal(barrier, inc=1, device_id=other, device_id_type=pl.DeviceIdType.MESH)
    pl.semaphore_wait(barrier, 3)

    sib_p_copy().start()
    for i in range(1, n // 2 + 1):
        sib_b_copy(shard(0, i)).start()
        if i < n // 2:
            sib_b_copy(shard(1, i)).start()
    sib_b_copy(place).start()

    def set_transposed(ref, span):
        high, low = split(ref[:depth, :window].T)
        pt_high[:window, span] = high
        pt_low[:window, span] = low
        pt_high[window:, span] = high[:near]
        pt_low[window:, span] = low[:near]

    set_transposed(b_ref, slice(0, depth))
    sib_p_copy().wait_recv()
    set_transposed(sib_b, slice(depth, 2 * depth))

    def set_part(d, q):
        def product(lhs, cols):
            both = jnp.concatenate([b_ref[:depth, cols], sib_b[:, cols]], axis=0)
            return dot3(pt_high[lhs, :], pt_low[lhs, :], *split(both))

        part[d, :near_rows] = product(near_span(d, q), columns(q))
        part[d, near_rows:] = product(far_span(d), far_columns(q))

    @pl.loop(0, 2)
    def _(d):
        sib_b_copy(shard(d, 1)).wait_recv()
        set_part(d, shard(d, 1))
        buf[d, 0] = part[d]
        for u in range(SUB):
            red_copy(d, 0, u).start()

    for i in range(2, n // 2 + 1):
        sib_b_copy(shard(0, i)).wait_recv()
        if i < n // 2:
            sib_b_copy(shard(1, i)).wait_recv()
    sib_b_copy(place).wait_recv()
    high, low = split(b_ref[:depth, :window])
    p_high[:, :window] = high
    p_low[:, :window] = low
    p_high[:, window:] = high[:, :near]
    p_low[:, window:] = low[:, :near]
    out_ref[:, :window] = jnp.zeros((depth, window), jnp.float32)
    for k in range(n):
        here = slice(k * width, (k + 1) * width)
        one = b_ref[depth : depth + 1, here]
        row_ref[here, :] = jnp.broadcast_to(one, (width, width)).T
    row_ref[window:, :] = row_ref[:near, :]
    for d in range(2):
        near_energy = b_ref[depth : depth + 1, columns(place)]
        far_energy = b_ref[depth : depth + 1, far_columns(place)]
        energy[d, :near_rows] = row_ref[near_span(d, place), :] + near_energy
        energy[d, near_rows:] = row_ref[far_span(d), :] + far_energy

    @pl.loop(1, n - 1)
    def _(s):
        @pl.loop(0, 2)
        def _(d):
            set_part(d, shard(d, s + 1))
        for u in range(SUB):
            for d in range(2):
                red_copy(d, s - 1, u).wait_recv()
                buf[d, s, sub(u)] += part[d, sub(u)]
                red_copy(d, s, u).start()

    @pl.loop(0, 2)
    def _(d):
        set_part(d, place)
    for u in range(SUB):
        for d in range(2):
            red_copy(d, n - 2, u).wait_recv()
            integrals = buf[d, n - 1, sub(u)] + part[d, sub(u)]
            amp[place, core, d, sub(u)] = os_scale * integrals / energy[d, sub(u)]
            gat_copy(d, 0, u, place).start()
            sib_a_copy(d, 0, u, place).start()

    def density(q):
        far = jnp.zeros((depth, width), jnp.float32)
        for j in range(4):
            span = slice(j * far_rows, (j + 1) * far_rows)
            far += dot3(
                p_high[:, span], p_low[:, span], *split(amp[q, j // 2, j % 2, near_rows:]))
        out_ref[:, far_columns(q)] = far
        block = jnp.concatenate([amp[q, j // 2, j % 2, :near_rows] for j in range(4)], axis=0)
        high, low = split(block)
        span = pl.ds(pl.multiple_of(q * width, width), near)
        out_ref[:, columns(q)] += dot3(p_high[:, span], p_low[:, span], high, low)
        q_high, q_low = p_high[:, columns(q)], p_low[:, columns(q)]
        for i in range(1, n // 2):
            there = slice(i * width, (i + 1) * width)
            out_ref[:, columns((q + i) % n)] += dot3(
                q_high, q_low, high[there].T, low[there].T)

    def finish(d, j):
        q = shard(d, j)
        for u in range(SUB):
            sib_a_arrival(d, j, u, q).wait_recv()
            sib_a_arrival(1 - d, (n - j) % n, u, q).wait_recv()
        density(q)

    middle = n // 2

    @pl.loop(0, n - 1)
    def _(s):
        for u in range(SUB):
            for d in range(2):
                q = shard(d, s + 1)
                gat_copy(d, s, u, q).wait_recv()

                @pl.when(s < n - 2)
                def _():
                    gat_copy(d, s + 1, u, q).start()

                sib_a_copy(d, s + 1, u, q).start()

            if u == 0:
                @pl.when((s == 1) | (s >= middle))
                def _():
                    finish(0, (n - s) % (n - 1))
            elif u == SUB // 2:
                @pl.when(s > middle)
                def _():
                    finish(1, n - s)

    @pl.loop(0, 2)
    def _(d):
        finish(d, 1)

    sib_p_copy().wait_send()

    @pl.loop(0, n)
    def _(q):
        sib_b_copy(q).wait_send()

    for d in range(2):
        for u in range(SUB):
            @pl.loop(0, n - 1)
            def _(s):
                red_copy(d, s, u).wait_send()
                gat_copy(d, s, u, shard(d, s)).wait_send()

            @pl.loop(0, n)
            def _(t):
                sib_a_copy(d, t, u, shard(d, t)).wait_send()


def by_rows(factors, occupied_energy, virtual_energy, batch_orbitals, panel_order):
    n = lax.axis_size("pair")
    depth, total = factors.shape
    window = panel_order.shape[0] * PANEL
    width = window // n
    near = (n // 2 + 1) * width
    stream = (near + window) // 4
    dma = pltpu.SemaphoreType.DMA
    smem, vmem = pl.BlockSpec(memory_space=pltpu.SMEM), pl.BlockSpec(memory_space=pltpu.VMEM)
    place, ordered = pl.pallas_call(
        sort_kernel,
        out_shape=[
            jax.ShapeDtypeStruct((total // PANEL,), jnp.int32),
            jax.ShapeDtypeStruct((depth + 8, total), jnp.float32),
        ],
        in_specs=[smem] * 3 + [vmem] * 2,
        out_specs=[smem, vmem],
        scratch_shapes=[
            pltpu.SMEM((total // PANEL + 1,), jnp.int32),
            pltpu.VMEM((1, total), jnp.float32),
        ],
    )(panel_order, batch_orbitals, occupied_energy, virtual_energy.reshape(1, -1), factors)
    density = pl.pallas_call(
        functools.partial(ring_kernel, n),
        out_shape=jax.ShapeDtypeStruct((depth, total), jnp.float32),
        in_specs=[vmem],
        out_specs=vmem,
        scratch_shapes=[
            pltpu.VMEM((window + near, width), jnp.float32),
            pltpu.VMEM((depth, total), jnp.float32),
            pltpu.VMEM((window + near, 2 * depth), jnp.bfloat16),
            pltpu.VMEM((window + near, 2 * depth), jnp.bfloat16),
            pltpu.VMEM((depth, window + near), jnp.bfloat16),
            pltpu.VMEM((depth, window + near), jnp.bfloat16),
            pltpu.VMEM((2, stream, width), jnp.float32),
            pltpu.VMEM((2, stream, width), jnp.float32),
            pltpu.VMEM((2, n, stream, width), jnp.float32),
            pltpu.VMEM((n, 2, 2, stream, width), jnp.float32),
            dma, dma, dma((n,)), dma((n,)),
            dma((2, n - 1, SUB)), dma((2, n - 1, SUB)),
            dma((2, n - 1, SUB)), dma((2, n - 1, SUB)),
            dma((2, n, SUB)), dma((2, n, SUB)),
        ],
        compiler_params=pltpu.CompilerParams(
            collective_id=0, has_side_effects=True, vmem_limit_bytes=48 * 1024 * 1024
        ),
        cost_estimate=pl.CostEstimate(
            flops=12 * depth * window * total, bytes_accessed=8 * depth * total, transcendentals=0
        ),
    )(ordered)
    return pl.pallas_call(
        unsort_kernel,
        out_shape=jax.ShapeDtypeStruct((depth, total), jnp.float32),
        grid=(4,),
        in_specs=[smem, pl.BlockSpec((depth // 4, total), lambda i: (i, 0))],
        out_specs=pl.BlockSpec((depth // 4, total), lambda i: (i, 0)),
    )(place, density)


def on_device(factors, occupied_energy, virtual_energy, batch_orbitals, panel_order):
    window = panel_order.shape[0] * PANEL
    n = lax.axis_size("pair")
    fits = n % 2 == 0 and window == 2 * PANEL * n and factors.shape[1] == 2 * window
    plan = by_rows if fits else by_columns
    return plan(factors, occupied_energy, virtual_energy, batch_orbitals, panel_order)


def solution(mesh):
    in_specs = (
        P(("groups", "pair", "aux"), None),
        P("groups"),
        P("groups"),
        P("groups"),
        P("groups"),
    )
    out_specs = P(("groups", "pair", "aux"), None)
    return jax.shard_map(
        on_device, mesh=mesh, in_specs=in_specs, out_specs=out_specs, check_vma=False
    )
```
